32 devices in a mesh: span: 16 (over z, x, core), row: 2 (over y).
Axes of the slice: x: 2, y: 2, z: 4, core: 2. Of those that a mesh axis runs over, the one named last changes fastest.
Arguments:
- features: bfloat16 [16, 4, 16, 32, 128], P('span', None, 'row'), may hold values from -6 to 6
- clip_lengths: int32 [4], replicated, may hold values from 1 to 8, 16 in all
- clip_order: int32 [4], replicated, may hold values from 0 to 3, each once
- weight_a: bfloat16 [3, 3, 3, 128, 128], replicated, may hold values from -0.109375 to 0.109375
- bias_a: float32 [128], replicated, may hold values from -3 to 3
- weight_b: bfloat16 [3, 3, 3, 128, 128], replicated, may hold values from -0.109375 to 0.109375
- bias_b: float32 [128], replicated, may hold values from -3 to 3
- weight_down: bfloat16 [3, 3, 3, 128, 128], replicated, may hold values from -0.109375 to 0.109375
- bias_down: float32 [128], replicated, may hold values from -3 to 3
Outputs:
- patch_tokens: bfloat16 [16, 2, 4, 8, 512], P('span', None, 'row')
The draws below stay inside these ranges and needn't reach their ends.
Inputs may be any that keep to these rules, and one draw needn't show every extreme that they name: `clip_lengths`: the lengths sum to 16. `clip_order`: each clip appears once.
All inputs are finite; a program needn't handle non-finite values.
Results may differ from the reference program's by a relative error of at most 0.0051.
Values may be sent and summed in bfloat16 or wider, within the bound.
A program may use at most 64 MiB of HBM per device.

```python
import math
import jax
import jax.numpy as jnp
import numpy as np
from jax import lax

C = 128
FRAMES = 4
COLS = 32
ROWS = 16
CLIPS = 4
MAXC = 8
N_SPAN = 16


def steps_of(rng, shape, shards, low, largest):
    gain = 1.0
    for dim, blocks in shards:
        draws = jax.random.uniform(jax.random.fold_in(jax.random.fold_in(rng, 6), dim), (blocks,), jnp.float32, low / len(shards), largest / len(shards))
        gain = gain * jnp.repeat(jnp.exp(draws), shape[dim] // blocks).reshape((-1,) + (1,) * (len(shape) - 1 - dim))
    return gain


def length_profile(amount, total, bound, skew):
    portions = [(1 << 20) // math.isqrt(rank ** skew) + 1 for rank in range(2, amount + 1)]
    rest, holding = total - bound - (amount - 1), [1] * (amount - 1)
    while rest > 0:
        candidates = [i for i in range(amount - 1) if holding[i] < bound]
        mass, left = sum([portions[i] for i in candidates]), rest
        for i in candidates:
            more = min(bound - holding[i], max(1, left * portions[i] // mass), rest)
            holding[i] = holding[i] + more
            rest = rest - more
    return np.array([bound] + holding)


def uneven(own_key, amount, total, reach, skew):
    if amount == 2:
        one = jax.random.randint(own_key, (), max(1, total - reach), min(reach, total - 1) + 1)
        return jnp.stack([one, total - one])
    tallies = jnp.asarray(length_profile(amount, total, reach, skew), jnp.int32)
    pairs = (amount - 1) // 2
    donor, sink = tallies[1:1 + 2 * pairs:2], tallies[2:2 + 2 * pairs:2]
    slack = jnp.minimum(donor - 1, reach - sink)
    passed = jax.random.randint(jax.random.fold_in(own_key, 1), (pairs,), 0, 1 << 20) % (slack + 1)
    tallies = tallies.at[1:1 + 2 * pairs:2].set(donor - passed).at[2:2 + 2 * pairs:2].set(sink + passed)
    return tallies[jax.random.permutation(jax.random.fold_in(own_key, 2), amount)]


def noise(stream_key, dims, width, reach, shards=(), kind=jnp.bfloat16):
    drawn = jax.random.normal(stream_key, dims, jnp.float32) * width
    if len(shards) > 0:
        drawn = steps_of(stream_key, dims, shards, -0.22, 0.18) * drawn
    return jnp.clip(drawn, min=-reach, max=reach).astype(kind)


def setup_inputs(seed: int = 0) -> dict:
    key_list = jax.random.split(jax.random.key(seed), 10)
    features = noise(key_list[0], (N_SPAN, FRAMES, ROWS, COLS, C), 1.0, 6.0, ((0, 16), (2, 2)))
    clip_lengths = uneven(key_list[1], CLIPS, N_SPAN, MAXC, 2).astype(jnp.int32)
    clip_order = jax.random.permutation(key_list[2], CLIPS).astype(jnp.int32)
    weight_a = noise(key_list[3], (3, 3, 3, C, C), (27 * C) ** -0.5, 0.109375)
    bias_a = noise(key_list[4], (C,), 0.5, 3.0, (), jnp.float32)
    weight_b = noise(key_list[5], (3, 3, 3, C, C), (27 * C) ** -0.5, 0.109375)
    bias_b = noise(key_list[6], (C,), 0.5, 3.0, (), jnp.float32)
    weight_down = noise(key_list[7], (3, 3, 3, C, C), (27 * C) ** -0.5, 0.109375)
    bias_down = noise(key_list[8], (C,), 0.5, 3.0, (), jnp.float32)
    return {"features": features, "clip_lengths": clip_lengths, "clip_order": clip_order, "weight_a": weight_a, "bias_a": bias_a, "weight_b": weight_b, "bias_b": bias_b, "weight_down": weight_down, "bias_down": bias_down}


def positions(clip_lengths, clip_order, slots):
    clips = clip_lengths.shape[0]
    pick = clip_order[:, None] == jnp.arange(clips, dtype=jnp.int32)[None, :]
    ordered = jnp.sum(jnp.where(pick, clip_lengths[None, :], 0), axis=1).astype(jnp.int32)
    ends = jnp.cumsum(ordered).astype(jnp.int32)
    starts = (ends - ordered).astype(jnp.int32)
    began = jnp.where(starts[None, :] <= slots[:, None], starts[None, :], 0)
    return (slots - jnp.max(began, axis=1)).astype(jnp.int32)


def with_context(field, keep):
    earlier = jnp.concatenate([jnp.zeros_like(field[:1, -2:]), field[:-1, -2:]], axis=0)
    earlier = earlier * keep[:, None, None, None, None]
    return jnp.concatenate([earlier, field], axis=1)


def convolve(extended, weight, stride):
    result = lax.conv_general_dilated(
        extended[None].astype(jnp.float32), weight.astype(jnp.float32),
        (stride, stride, stride), ((0, 0), (1, 1), (1, 1)),
        dimension_numbers=("NDHWC", "DHWIO", "NDHWC"),
        precision=lax.Precision.HIGHEST)
    return result[0]


def reference(features, clip_lengths, clip_order, weight_a, bias_a, weight_b, bias_b, weight_down, bias_down):
    slots = jnp.arange(features.shape[0], dtype=jnp.int32)
    position = positions(clip_lengths, clip_order, slots)
    keep = (position > 0).astype(jnp.bfloat16)
    first_in = with_context(features, keep)
    hidden = lax.map(lambda ext: jax.nn.silu(convolve(ext, weight_a, 1) + bias_a).astype(jnp.bfloat16), first_in)
    second_in = with_context(hidden, keep)

    def residual(pair):
        return (pair[0].astype(jnp.float32) + convolve(pair[1], weight_b, 1) + bias_b).astype(jnp.bfloat16)

    mixed = lax.map(residual, (features, second_in))
    third_in = with_context(mixed, keep)
    latent = lax.map(lambda ext: (convolve(ext, weight_down, 2) + bias_down).astype(jnp.bfloat16), third_in)
    slots_n, frames_n, rows_n, cols_n, chans = latent.shape
    grouped = latent.reshape(slots_n, frames_n, rows_n // 2, 2, cols_n // 2, 2, chans)
    grouped = jnp.transpose(grouped, (0, 1, 2, 4, 3, 5, 6))
    return grouped.reshape(slots_n, frames_n, rows_n // 2, cols_n // 2, 4 * chans)
```

```python
import functools

import jax
import jax.numpy as jnp
from jax import lax
from jax.experimental import pallas as pl
from jax.experimental.pallas import tpu as pltpu
from jax.sharding import PartitionSpec as P

MESH = pl.DeviceIdType.MESH
UP = 3
LOW = 2
BF16 = jnp.bfloat16
F32 = jnp.float32


def kernel(
    spans,
    rows_n,
    x_hbm,
    lengths,
    order,
    wa_hbm,
    ba,
    wb_hbm,
    bb,
    wd_hbm,
    bd,
    out,
    xs,
    hs,
    ms,
    wa,
    wb,
    wd,
    cells,
    send_sem,
    recv_sem,
    load_sem,
):
    s = lax.axis_index("span")
    r = lax.axis_index("row")
    height, cols, chans = x_hbm.shape[2], x_hbm.shape[3], x_hbm.shape[4]
    hid_rows = height + UP
    mix_rows = height + 1

    first_s, last_s = s == 0, s == spans - 1
    first_r, last_r = r == 0, r == rows_n - 1
    no = jnp.logical_not
    both = jnp.logical_and
    s_to, r_to, r_back = (
        jnp.minimum(s + 1, spans - 1),
        jnp.minimum(r + 1, rows_n - 1),
        jnp.maximum(r - 1, 0),
    )
    s_from = jnp.maximum(s - 1, 0)
    kinds = [
        ((s, r_to), no(last_r), no(first_r), (s, r_back)),
        ((s, r_back), no(first_r), no(last_r), (s, r_to)),
        ((s_to, r), no(last_s), no(first_s), (s_from, r)),
        (
            (s_to, r_to),
            both(no(last_s), no(last_r)),
            both(no(first_s), no(first_r)),
            (s_from, r_back),
        ),
        (
            (s_to, r_back),
            both(no(last_s), no(first_r)),
            both(no(first_s), no(last_r)),
            (s_from, r_to),
        ),
    ]

    barrier = pltpu.get_barrier_semaphore()
    for _, _, receives, sender in kinds:

        @pl.when(receives)
        def _():
            pl.semaphore_signal(barrier, inc=1, device_id=sender, device_id_type=MESH)

    own = pltpu.make_async_copy(x_hbm.at[0], xs.at[2:6, UP : UP + height], load_sem.at[0])
    own.start()

    def paired(source, target, at):
        copies = []
        for o in range(2):
            copy = pltpu.make_async_copy(
                source,
                target.at[o : o + 3, :, :, :, o * chans : (o + 1) * chans],
                load_sem.at[at + o],
            )
            copy.start()
            copies.append(copy)
        return copies

    load_a = paired(wa_hbm, wa, 1)

    greeted = sum(sends.astype(jnp.int32) for _, sends, _, _ in kinds)
    pl.semaphore_wait(barrier, greeted)

    feats = x_hbm.at[0]
    routes = [
        (feats.at[:, height - UP : height], xs.at[2:6, 0:UP]),
        (feats.at[:, 0:LOW], xs.at[2:6, UP + height : UP + height + LOW]),
        (feats.at[2:4], xs.at[0:2, UP : UP + height]),
        (feats.at[2:4, height - UP : height], xs.at[0:2, 0:UP]),
        (feats.at[2:4, 0:LOW], xs.at[0:2, UP + height : UP + height + LOW]),
        (hs.at[4:6], hs.at[0:2]),
        (ms.at[4:6], ms.at[0:2]),
    ]
    kinds = kinds + [kinds[2], kinds[2]]

    def remote(k):
        return pltpu.make_async_remote_copy(
            src_ref=routes[k][0],
            dst_ref=routes[k][1],
            send_sem=send_sem.at[k],
            recv_sem=recv_sem.at[k],
            device_id=kinds[k][0],
            device_id_type=MESH,
        )

    def send(k):
        @pl.when(kinds[k][1])
        def _():
            remote(k).start()

    def sent(k):
        @pl.when(kinds[k][1])
        def _():
            remote(k).wait_send()

    def arrived(k):
        @pl.when(kinds[k][2])
        def _():
            remote(k).wait_recv()

    for k in range(5):
        send(k)

    load_b = paired(wb_hbm, wb, 3)
    load_d = []
    for w in range(3):
        copy = pltpu.make_async_copy(
            wd_hbm.at[:, :, w], wd.at[:, :, :, w * chans : (w + 1) * chans], load_sem.at[5 + w]
        )
        copy.start()
        load_d.append(copy)

    for target in (wa, wb):
        blank = jnp.zeros((3, 3, chans, chans), BF16)
        target[0, :, :, :, chans : 2 * chans] = blank
        target[3, :, :, :, 0:chans] = blank

    @pl.when(first_s)
    def _():
        for field in (xs, hs, ms):
            field[0:2] = jnp.zeros((2,) + field.shape[1:], BF16)

    @pl.when(first_r)
    def _():
        xs[:, 0:UP] = jnp.zeros((6, UP, cols, chans), BF16)

    @pl.when(last_r)
    def _():
        xs[:, UP + height :] = jnp.zeros((6, LOW, cols, chans), BF16)

    start = jnp.int32(0)
    keep = jnp.int32(1)
    for i in range(lengths.shape[0]):
        keep = jnp.where(start == s, 0, keep)
        start = start + lengths[order[i]]
    keep = keep.astype(F32)

    def gate(field):
        block = field[0:2]
        field[0:2] = (block.astype(F32) * keep).astype(BF16)

    def shifted(y0, y1, y2):
        col = lax.broadcasted_iota(jnp.int32, y1.shape, 0) % cols
        n = y1.shape[0]
        left = jnp.where(col == 0, 0.0, pltpu.roll(y0, 1, 0))
        right = jnp.where(col == cols - 1, 0.0, pltpu.roll(y2, n - 1, 0))
        return y1 + left + right

    def conv_pair(field, base, rows, weight):
        lhs = jnp.concatenate(
            [
                field[base + f, h : h + rows].reshape(rows * cols, chans)
                for f in range(4)
                for h in range(3)
            ],
            axis=1,
        )
        y = [
            jnp.dot(
                lhs,
                weight[:, :, w].reshape(12 * chans, 2 * chans),
                preferred_element_type=F32,
            )
            for w in range(3)
        ]
        return shifted(*y)

    def hidden_pair(base):
        y = conv_pair(xs, base, hid_rows, wa)
        for o in range(2):
            v = y[:, o * chans : (o + 1) * chans] + ba[...].reshape(1, chans)
            v = v / (1.0 + jnp.exp(-v))
            hs[base + 2 + o] = v.astype(BF16).reshape(hid_rows, cols, chans)

        @pl.when(first_r)
        def _():
            hs[base + 2 : base + 4, 0 : UP - 1] = jnp.zeros((2, UP - 1, cols, chans), BF16)

        @pl.when(last_r)
        def _():
            hs[base + 2 : base + 4, hid_rows - 1 :] = jnp.zeros((2, 1, cols, chans), BF16)

    def mixed_pair(base):
        y = conv_pair(hs, base, mix_rows, wb)
        for o in range(2):
            v = y[:, o * chans : (o + 1) * chans] + bb[...].reshape(1, chans)
            x = xs[base + 2 + o, UP - 1 : UP - 1 + mix_rows].reshape(mix_rows * cols, chans)
            v = x.astype(F32) + v
            ms[base + 2 + o] = v.astype(BF16).reshape(mix_rows, cols, chans)

        @pl.when(first_r)
        def _():
            ms[base + 2 : base + 4, 0:1] = jnp.zeros((2, 1, cols, chans), BF16)

    def down(j):
        high = height // 2
        lhs = jnp.concatenate(
            [
                jnp.concatenate([ms[2 * j + t, 2 * q + h] for q in range(high)], axis=0)
                for t in range(3)
                for h in range(3)
            ],
            axis=1,
        )
        y = jnp.dot(
            lhs, wd[...].reshape(9 * chans, 3 * chans), preferred_element_type=F32
        )
        y = shifted(*[y[:, w * chans : (w + 1) * chans] for w in range(3)])
        cells[...] = y + bd[...].reshape(1, chans)
        for i in range(high // 2):
            parts = []
            for a in range(2):
                for b in range(2):
                    at = (2 * i + a) * cols + 2 * b
                    parts.append(cells[pl.ds(at, cols // 4, stride=4), :])
            out[0, j, i] = jnp.concatenate(parts, axis=1).astype(BF16)

    own.wait()
    for copy in load_a:
        copy.wait()
    arrived(0)
    arrived(1)
    hidden_pair(2)
    send(5)
    for k in (2, 3, 4):
        arrived(k)
    gate(xs)
    hidden_pair(0)
    for copy in load_b:
        copy.wait()
    mixed_pair(2)
    send(6)
    arrived(5)
    gate(hs)
    mixed_pair(0)
    for copy in load_d:
        copy.wait()
    down(1)
    arrived(6)
    gate(ms)
    down(0)
    for k in range(7):
        sent(k)


def per_device(spans, rows_n, features, lengths, order, wa, ba, wb, bb, wd, bd):
    _, frames, height, cols, chans = features.shape
    hbm = pl.BlockSpec(memory_space=pl.ANY)
    vmem = pl.BlockSpec(memory_space=pltpu.VMEM)
    smem = pl.BlockSpec(memory_space=pltpu.SMEM)
    shape = (1, frames // 2, height // 4, cols // 4, 4 * chans)
    return pl.pallas_call(
        functools.partial(kernel, spans, rows_n),
        out_shape=jax.ShapeDtypeStruct(shape, BF16),
        in_specs=[hbm, smem, smem, hbm, vmem, hbm, vmem, hbm, vmem],
        out_specs=vmem,
        scratch_shapes=[
            pltpu.VMEM((frames + 2, height + UP + LOW, cols, chans), BF16),
            pltpu.VMEM((frames + 2, height + UP, cols, chans), BF16),
            pltpu.VMEM((frames + 2, height + 1, cols, chans), BF16),
            pltpu.VMEM((4, 3, 3, chans, 2 * chans), BF16),
            pltpu.VMEM((4, 3, 3, chans, 2 * chans), BF16),
            pltpu.VMEM((3, 3, chans, 3 * chans), BF16),
            pltpu.VMEM((height // 2 * cols, chans), F32),
            pltpu.SemaphoreType.DMA((7,)),
            pltpu.SemaphoreType.DMA((7,)),
            pltpu.SemaphoreType.DMA((8,)),
        ],
        compiler_params=pltpu.CompilerParams(
            collective_id=0, has_side_effects=True, vmem_limit_bytes=40 * 1024 * 1024
        ),
    )(features, lengths, order, wa, ba, wb, bb, wd, bd)


def solution(mesh):
    placed = (P("span", None, "row", None, None), P(), P(), P(), P(), P(), P(), P(), P())
    return jax.shard_map(
        functools.partial(per_device, mesh.shape["span"], mesh.shape["row"]),
        mesh=mesh,
        in_specs=placed,
        out_specs=P("span", None, "row", None, None),
        check_vma=False,
    )
```

```python
import functools

import jax
import jax.numpy as jnp
from jax import lax
from jax.experimental import pallas as pl
from jax.experimental.pallas import tpu as pltpu
from jax.sharding import PartitionSpec as P

MESH = pl.DeviceIdType.MESH
UP = 3
LOW = 2
BF16 = jnp.bfloat16
F32 = jnp.float32


def kernel(
    spans,
    rows_n,
    x_hbm,
    lengths_hbm,
    order_hbm,
    wa_hbm,
    ba_hbm,
    wb_hbm,
    bb_hbm,
    wd_hbm,
    bd_hbm,
    out,
    xs,
    hs,
    ms,
    wa,
    wb,
    wd,
    ba,
    bb,
    bd,
    lengths,
    order,
    cells,
    share,
    passed,
    send_sem,
    recv_sem,
    load_sem,
):
    s = lax.axis_index("span")
    r = lax.axis_index("row")
    height, cols, chans = x_hbm.shape[2], x_hbm.shape[3], x_hbm.shape[4]
    hid_rows = height + UP
    mix_rows = height + 1
    inner = UP + height - 2

    first_s, last_s = s == 0, s == spans - 1
    first_r, last_r = r == 0, r == rows_n - 1
    no = jnp.logical_not
    both = jnp.logical_and
    s_to, r_to, r_back = (
        jnp.minimum(s + 1, spans - 1),
        jnp.minimum(r + 1, rows_n - 1),
        jnp.maximum(r - 1, 0),
    )
    s_from = jnp.maximum(s - 1, 0)
    kinds = [
        ((s, r_to), no(last_r), no(first_r), (s, r_back)),
        ((s, r_back), no(first_r), no(last_r), (s, r_to)),
        ((s_to, r), no(last_s), no(first_s), (s_from, r)),
        (
            (s_to, r_to),
            both(no(last_s), no(last_r)),
            both(no(first_s), no(first_r)),
            (s_from, r_back),
        ),
        (
            (s_to, r_back),
            both(no(last_s), no(first_r)),
            both(no(first_s), no(last_r)),
            (s_from, r_to),
        ),
    ]

    barrier = pltpu.get_barrier_semaphore()
    for _, _, receives, sender in kinds:

        @pl.when(receives)
        def _():
            pl.semaphore_signal(barrier, inc=1, device_id=sender, device_id_type=MESH)

    used = [0]

    def load(source, target):
        copy = pltpu.make_async_copy(source, target, load_sem.at[used[0]])
        used[0] += 1
        copy.start()
        return copy

    def paired(source, target):
        return [
            load(source.at[t], target.at[t + o, :, :, :, o * chans : (o + 1) * chans])
            for t in range(3)
            for o in range(2)
        ]

    load_x = [load(x_hbm.at[0], xs.at[2:6, UP : UP + height])]
    load_a = paired(wa_hbm, wa) + [load(ba_hbm, ba)]
    load_i = [load(lengths_hbm, lengths), load(order_hbm, order)]

    def blank(target):
        zeros = jnp.zeros((3, 3, chans, chans), BF16)
        target[0, :, :, :, chans : 2 * chans] = zeros
        target[3, :, :, :, 0:chans] = zeros

    blank(wa)

    greeted = sum(sends.astype(jnp.int32) for _, sends, _, _ in kinds)
    pl.semaphore_wait(barrier, greeted)

    feats = x_hbm.at[0]
    routes = [
        (feats.at[:, height - UP : height], xs.at[2:6, 0:UP]),
        (feats.at[:, 0:LOW], xs.at[2:6, UP + height : UP + height + LOW]),
        (feats.at[2:4], xs.at[0:2, UP : UP + height]),
        (feats.at[2:4, height - UP : height], xs.at[0:2, 0:UP]),
        (feats.at[2:4, 0:LOW], xs.at[0:2, UP + height : UP + height + LOW]),
        (hs.at[4:6, UP:inner], hs.at[0:2, UP:inner]),
        (hs.at[4:6, 0:UP], hs.at[0:2, 0:UP]),
        (hs.at[4:6, inner:], hs.at[0:2, inner:]),
        (share, passed),
    ]
    kinds = kinds + 4 * [kinds[2]]

    def remote(k):
        return pltpu.make_async_remote_copy(
            src_ref=routes[k][0],
            dst_ref=routes[k][1],
            send_sem=send_sem.at[k],
            recv_sem=recv_sem.at[k],
            device_id=kinds[k][0],
            device_id_type=MESH,
        )

    def send(k):
        @pl.when(kinds[k][1])
        def _():
            remote(k).start()

    def sent(k):
        @pl.when(kinds[k][1])
        def _():
            remote(k).wait_send()

    def arrived(k):
        @pl.when(kinds[k][2])
        def _():
            remote(k).wait_recv()

    for k in range(5):
        send(k)

    load_b = paired(wb_hbm, wb) + [load(bb_hbm, bb)]
    load_d = [
        load(wd_hbm.at[:, :, w], wd.at[:, :, :, w * chans : (w + 1) * chans]) for w in range(3)
    ] + [load(bd_hbm, bd)]
    blank(wb)

    @pl.when(first_s)
    def _():
        for field in (xs, hs):
            field[0:2] = jnp.zeros((2,) + field.shape[1:], BF16)
        passed[...] = jnp.zeros(passed.shape, F32)

    @pl.when(first_r)
    def _():
        xs[:, 0:UP] = jnp.zeros((6, UP, cols, chans), BF16)

    @pl.when(last_r)
    def _():
        xs[:, UP + height :] = jnp.zeros((6, LOW, cols, chans), BF16)

    def waited(copies):
        for copy in copies:
            copy.wait()

    def shifted(y0, y1, y2):
        n, width = y1.shape
        col = lax.broadcasted_iota(jnp.int32, (n // cols, cols, width), 1).reshape(n, width)
        left = jnp.where(col == 0, 0.0, pltpu.roll(y0, 1, 0))
        right = jnp.where(col == cols - 1, 0.0, pltpu.roll(y2, n - 1, 0))
        return y1 + left + right

    def stacked(field, frame, parts):
        got = [field[frame, lo:hi].reshape((hi - lo) * cols, chans) for lo, hi in parts]
        return got[0] if len(got) == 1 else jnp.concatenate(got, axis=0)

    def conv_pair(field, base, parts, weight):
        lhs = jnp.concatenate(
            [
                stacked(field, base + f, [(lo + h, hi + h) for lo, hi in parts])
                for f in range(4)
                for h in range(3)
            ],
            axis=1,
        )
        y = [
            jnp.dot(
                lhs,
                weight[:, :, w].reshape(12 * chans, 2 * chans),
                preferred_element_type=F32,
            )
            for w in range(3)
        ]
        return shifted(*y)

    def hidden_pair(base, parts):
        y = conv_pair(xs, base, parts, wa)
        for o in range(2):
            v = y[:, o * chans : (o + 1) * chans] + ba[...].reshape(1, chans)
            v = (v / (1.0 + jnp.exp(-v))).astype(BF16)
            at = 0
            for lo, hi in parts:
                n = (hi - lo) * cols
                hs[base + 2 + o, lo:hi] = v[at : at + n].reshape(hi - lo, cols, chans)
                at += n

    def hidden_rim(base):
        @pl.when(first_r)
        def _():
            hs[base + 2 : base + 4, 0 : UP - 1] = jnp.zeros((2, UP - 1, cols, chans), BF16)

        @pl.when(last_r)
        def _():
            hs[base + 2 : base + 4, hid_rows - 1 :] = jnp.zeros((2, 1, cols, chans), BF16)

    def mixed_pair(base):
        y = conv_pair(hs, base, [(0, mix_rows)], wb)
        for o in range(2):
            v = y[:, o * chans : (o + 1) * chans] + bb[...].reshape(1, chans)
            x = xs[base + 2 + o, UP - 1 : UP - 1 + mix_rows].reshape(mix_rows * cols, chans)
            v = x.astype(F32) + v
            ms[base + o] = v.astype(BF16).reshape(mix_rows, cols, chans)

        @pl.when(first_r)
        def _():
            ms[base : base + 2, 0:1] = jnp.zeros((2, 1, cols, chans), BF16)

    high = height // 2

    def down(base, first, count):
        lhs = jnp.concatenate(
            [
                jnp.concatenate([ms[base + t, 2 * q + h] for q in range(high)], axis=0)
                for t in range(count)
                for h in range(3)
            ],
            axis=1,
        )
        y = jnp.dot(
            lhs,
            wd[first : first + count].reshape(3 * count * chans, 3 * chans),
            preferred_element_type=F32,
        )
        return shifted(*[y[:, w * chans : (w + 1) * chans] for w in range(3)])

    def emit(j, extra):
        for i in range(high // 2):
            got = []
            for a in range(2):
                for b in range(2):
                    row = 2 * i + a
                    v = cells[j, pl.ds(row * cols + 2 * b, cols // 4, stride=4), :]
                    if extra is not None:
                        late = passed[pl.ds(row * (cols // 2) + b, cols // 4, stride=2), :]
                        v = v + late * extra
                    got.append(v)
            out[0, j, i] = jnp.concatenate(got, axis=1).astype(BF16)

    waited(load_x)
    waited(load_a)
    hidden_pair(2, [(UP, inner)])
    send(5)
    arrived(0)
    arrived(1)
    hidden_pair(2, [(0, UP), (inner, hid_rows)])
    hidden_rim(2)
    send(6)
    send(7)

    waited(load_i)
    start = jnp.int32(0)
    keep = jnp.int32(1)
    for i in range(lengths.shape[0]):
        keep = jnp.where(start == s, 0, keep)
        start = start + lengths[order[i]]
    keep = keep.astype(F32)

    def gate(field):
        block = field[0:2]
        field[0:2] = (block.astype(F32) * keep).astype(BF16)

    for k in (2, 3, 4):
        arrived(k)
    gate(xs)
    hidden_pair(0, [(0, hid_rows)])
    hidden_rim(0)
    waited(load_b)
    mixed_pair(2)
    waited(load_d)
    cells[0] = down(2, 0, 2)
    share[...] = cells[0, pl.ds(0, high * cols // 2, stride=2), :]
    send(8)
    for k in (5, 6, 7):
        arrived(k)
    gate(hs)
    mixed_pair(0)
    bias = bd[...].reshape(1, chans)
    cells[1] = down(0, 0, 3) + bias
    emit(1, None)
    cells[0] = down(0, 2, 1) + bias
    arrived(8)
    emit(0, keep)
    for k in range(9):
        sent(k)


def per_device(spans, rows_n, features, lengths, order, wa, ba, wb, bb, wd, bd):
    _, frames, height, cols, chans = features.shape
    hbm = pl.BlockSpec(memory_space=pltpu.HBM)
    vmem = pl.BlockSpec(memory_space=pltpu.VMEM)
    shape = (1, frames // 2, height // 4, cols // 4, 4 * chans)
    return pl.pallas_call(
        functools.partial(kernel, spans, rows_n),
        out_shape=jax.ShapeDtypeStruct(shape, BF16),
        in_specs=[hbm] * 9,
        out_specs=vmem,
        scratch_shapes=[
            pltpu.VMEM((frames + 2, height + UP + LOW, cols, chans), BF16),
            pltpu.VMEM((frames + 2, height + UP, cols, chans), BF16),
            pltpu.VMEM((frames, height + 1, cols, chans), BF16),
            pltpu.VMEM((4, 3, 3, chans, 2 * chans), BF16),
            pltpu.VMEM((4, 3, 3, chans, 2 * chans), BF16),
            pltpu.VMEM((3, 3, chans, 3 * chans), BF16),
            pltpu.VMEM((chans,), F32),
            pltpu.VMEM((chans,), F32),
            pltpu.VMEM((chans,), F32),
            pltpu.SMEM(lengths.shape, jnp.int32),
            pltpu.SMEM(order.shape, jnp.int32),
            pltpu.VMEM((2, height // 2 * cols, chans), F32),
            pltpu.VMEM((height // 4 * cols, chans), F32),
            pltpu.VMEM((height // 4 * cols, chans), F32),
            pltpu.SemaphoreType.DMA((9,)),
            pltpu.SemaphoreType.DMA((9,)),
            pltpu.SemaphoreType.DMA((22,)),
        ],
        compiler_params=pltpu.CompilerParams(
            collective_id=0, has_side_effects=True, vmem_limit_bytes=64 * 1024 * 1024
        ),
    )(features, lengths, order, wa, ba, wb, bb, wd, bd)


def solution(mesh):
    placed = (P("span", None, "row", None, None), P(), P(), P(), P(), P(), P(), P(), P())
    return jax.shard_map(
        functools.partial(per_device, mesh.shape["span"], mesh.shape["row"]),
        mesh=mesh,
        in_specs=placed,
        out_specs=P("span", None, "row", None, None),
        check_vma=False,
    )
```

```python
import functools

import jax
import jax.numpy as jnp
from jax import lax
from jax.experimental import pallas as pl
from jax.experimental.pallas import tpu as pltpu
from jax.sharding import PartitionSpec as P

MESH = pl.DeviceIdType.MESH
UP = 3
LOW = 2
GROUP = 3
BF16 = jnp.bfloat16
F32 = jnp.float32


def kernel(
    spans,
    rows_n,
    x_hbm,
    lengths_hbm,
    order_hbm,
    wa_hbm,
    ba_hbm,
    wb_hbm,
    bb_hbm,
    wd_hbm,
    bd_hbm,
    out,
    xs,
    hs,
    ms,
    wa,
    wb,
    wd,
    ba,
    bb,
    bd,
    lengths,
    order,
    cells,
    share,
    passed,
    send_sem,
    recv_sem,
    load_sem,
):
    s = lax.axis_index("span")
    r = lax.axis_index("row")
    height, cols, chans = x_hbm.shape[2], x_hbm.shape[3], x_hbm.shape[4]
    hid_rows = height + UP
    mix_rows = height + 1
    inner = UP + height - 2

    first_s, last_s = s == 0, s == spans - 1
    first_r, last_r = r == 0, r == rows_n - 1
    no = jnp.logical_not
    both = jnp.logical_and
    s_to, r_to, r_back = (
        jnp.minimum(s + 1, spans - 1),
        jnp.minimum(r + 1, rows_n - 1),
        jnp.maximum(r - 1, 0),
    )
    s_from = jnp.maximum(s - 1, 0)
    kinds = [
        ((s, r_to), no(last_r), no(first_r), (s, r_back)),
        ((s, r_back), no(first_r), no(last_r), (s, r_to)),
        ((s_to, r), no(last_s), no(first_s), (s_from, r)),
        (
            (s_to, r_to),
            both(no(last_s), no(last_r)),
            both(no(first_s), no(first_r)),
            (s_from, r_back),
        ),
        (
            (s_to, r_back),
            both(no(last_s), no(first_r)),
            both(no(first_s), no(last_r)),
            (s_from, r_to),
        ),
    ]

    barrier = pltpu.get_barrier_semaphore()
    for _, _, receives, sender in kinds:

        @pl.when(receives)
        def _():
            pl.semaphore_signal(barrier, inc=1, device_id=sender, device_id_type=MESH)

    used = [0]

    def load(source, target):
        copy = pltpu.make_async_copy(source, target, load_sem.at[used[0]])
        used[0] += 1
        copy.start()
        return copy

    def paired(source, target):
        return [
            load(source.at[t], target.at[t + o, :, :, :, o * chans : (o + 1) * chans])
            for t in range(3)
            for o in range(2)
        ]

    load_x = [load(x_hbm.at[0], xs.at[2:6, UP : UP + height])]
    load_a = paired(wa_hbm, wa) + [load(ba_hbm, ba)]
    load_i = [load(lengths_hbm, lengths), load(order_hbm, order)]

    def blank(target):
        zeros = jnp.zeros((3, 3, chans, chans), BF16)
        target[0, :, :, :, chans : 2 * chans] = zeros
        target[3, :, :, :, 0:chans] = zeros

    blank(wa)

    greeted = sum(sends.astype(jnp.int32) for _, sends, _, _ in kinds)
    pl.semaphore_wait(barrier, greeted)

    feats = x_hbm.at[0]
    routes = [
        (feats.at[:, height - UP : height], xs.at[2:6, 0:UP]),
        (feats.at[:, 0:LOW], xs.at[2:6, UP + height : UP + height + LOW]),
        (feats.at[2:4], xs.at[0:2, UP : UP + height]),
        (feats.at[2:4, height - UP : height], xs.at[0:2, 0:UP]),
        (feats.at[2:4, 0:LOW], xs.at[0:2, UP + height : UP + height + LOW]),
        (hs.at[4:6, UP:inner], hs.at[0:2, UP:inner]),
        (hs.at[4:6, 0:UP], hs.at[0:2, 0:UP]),
        (hs.at[4:6, inner:hid_rows], hs.at[0:2, inner:hid_rows]),
        (share, passed),
    ]
    kinds = kinds + 4 * [kinds[2]]

    def remote(k):
        return pltpu.make_async_remote_copy(
            src_ref=routes[k][0],
            dst_ref=routes[k][1],
            send_sem=send_sem.at[k],
            recv_sem=recv_sem.at[k],
            device_id=kinds[k][0],
            device_id_type=MESH,
        )

    def send(k):
        @pl.when(kinds[k][1])
        def _():
            remote(k).start()

    def sent(k):
        @pl.when(kinds[k][1])
        def _():
            remote(k).wait_send()

    def arrived(k):
        @pl.when(kinds[k][2])
        def _():
            remote(k).wait_recv()

    for k in range(5):
        send(k)

    load_b = paired(wb_hbm, wb) + [load(bb_hbm, bb)]
    load_d = [
        load(wd_hbm.at[:, :, w], wd.at[:, :, :, w * chans : (w + 1) * chans]) for w in range(3)
    ] + [load(bd_hbm, bd)]
    blank(wb)

    @pl.when(first_s)
    def _():
        for field in (xs, hs):
            field[0:2] = jnp.zeros((2,) + field.shape[1:], BF16)
        passed[...] = jnp.zeros(passed.shape, F32)

    @pl.when(first_r)
    def _():
        xs[:, 0:UP] = jnp.zeros((6, UP, cols, chans), BF16)

    @pl.when(last_r)
    def _():
        xs[:, UP + height : UP + height + LOW] = jnp.zeros((6, LOW, cols, chans), BF16)

    spare = xs.shape[1] - (UP + height + LOW)
    xs[:, UP + height + LOW :] = jnp.zeros((6, spare, cols, chans), BF16)

    def waited(copies):
        for copy in copies:
            copy.wait()

    def shifted(y0, y1, y2):
        n, width = y1.shape
        col = lax.broadcasted_iota(jnp.int32, (n // cols, cols, width), 1).reshape(n, width)
        left = jnp.where(col == 0, 0.0, pltpu.roll(y0, 1, 0))
        right = jnp.where(col == cols - 1, 0.0, pltpu.roll(y2, n - 1, 0))
        return y1 + left + right

    def stacked(field, frame, parts):
        got = [field[frame, pl.ds(lo, n)].reshape(n * cols, chans) for lo, n in parts]
        return got[0] if len(got) == 1 else jnp.concatenate(got, axis=0)

    def conv_pair(field, base, parts, weight):
        lhs = jnp.concatenate(
            [
                stacked(field, base + f, [(lo + h, n) for lo, n in parts])
                for f in range(4)
                for h in range(3)
            ],
            axis=1,
        )
        y = [
            jnp.dot(
                lhs,
                weight[:, :, w].reshape(12 * chans, 2 * chans),
                preferred_element_type=F32,
            )
            for w in range(3)
        ]
        return shifted(*y)

    def hidden_pair(base, parts):
        y = conv_pair(xs, base, parts, wa)
        for o in range(2):
            v = y[:, o * chans : (o + 1) * chans] + ba[...].reshape(1, chans)
            v = (v / (1.0 + jnp.exp(-v))).astype(BF16)
            at = 0
            for lo, n in parts:
                hs[base + 2 + o, pl.ds(lo, n)] = v[at : at + n * cols].reshape(n, cols, chans)
                at += n * cols

    def hidden_rim(base):
        @pl.when(first_r)
        def _():
            hs[base + 2 : base + 4, 0 : UP - 1] = jnp.zeros((2, UP - 1, cols, chans), BF16)

        @pl.when(last_r)
        def _():
            hs[base + 2 : base + 4, hid_rows - 1 : hid_rows] = jnp.zeros((2, 1, cols, chans), BF16)

    def mixed_pair(base):
        y = conv_pair(hs, base, [(0, mix_rows)], wb)
        for o in range(2):
            v = y[:, o * chans : (o + 1) * chans] + bb[...].reshape(1, chans)
            x = xs[base + 2 + o, UP - 1 : UP - 1 + mix_rows].reshape(mix_rows * cols, chans)
            v = x.astype(F32) + v
            ms[base + o] = v.astype(BF16).reshape(mix_rows, cols, chans)

        @pl.when(first_r)
        def _():
            for o in range(2):
                ms[base + o, 0:1] = jnp.zeros((1, cols, chans), BF16)

    high = height // 2

    def down(base, first, count):
        lhs = jnp.concatenate(
            [
                jnp.concatenate([ms[base + t, 2 * q + h] for q in range(high)], axis=0)
                for t in range(count)
                for h in range(3)
            ],
            axis=1,
        )
        y = jnp.dot(
            lhs,
            wd[first : first + count].reshape(3 * count * chans, 3 * chans),
            preferred_element_type=F32,
        )
        return shifted(*[y[:, w * chans : (w + 1) * chans] for w in range(3)])

    def emit(j, extra):
        for i in range(high // 2):
            got = []
            for a in range(2):
                for b in range(2):
                    row = 2 * i + a
                    v = cells[j, pl.ds(row * cols + 2 * b, cols // 4, stride=4), :]
                    if extra is not None:
                        late = passed[pl.ds(row * (cols // 2) + b, cols // 4, stride=2), :]
                        v = v + late * extra
                    got.append(v)
            out[0, j, i] = jnp.concatenate(got, axis=1)

    waited(load_x)
    waited(load_a)
    waited(load_i)
    start = jnp.int32(0)
    keep = jnp.int32(1)
    for i in range(lengths.shape[0]):
        keep = jnp.where(start == s, 0, keep)
        start = start + lengths[order[i]]
    keep = keep.astype(F32)

    def gate(field):
        block = field[0:2]
        field[0:2] = (block.astype(F32) * keep).astype(BF16)

    @pl.loop(0, 4)
    def _(i):
        @pl.when(i == 1)
        def _():
            arrived(0)
            arrived(1)

        @pl.when(i == 2)
        def _():
            for k in (2, 3, 4):
                arrived(k)
            gate(xs)

        outer = i % 2
        low = UP - GROUP * outer
        up = UP + GROUP + GROUP * outer
        hidden_pair(2 - 2 * (i // 2), [(low, GROUP), (up, GROUP)])

        @pl.when(i == 0)
        def _():
            send(5)

        @pl.when(i == 1)
        def _():
            hidden_rim(2)
            send(6)
            send(7)

        @pl.when(i == 3)
        def _():
            hidden_rim(0)

    waited(load_b)

    @pl.loop(0, 2)
    def _(i):
        @pl.when(i == 1)
        def _():
            for k in (5, 6, 7):
                arrived(k)
            gate(hs)

        mixed_pair(2 - 2 * i)

        @pl.when(i == 0)
        def _():
            waited(load_d)
            cells[0] = down(2, 0, 2)
            share[...] = cells[0, pl.ds(0, high * cols // 2, stride=2), :]
            send(8)

    bias = bd[...].reshape(1, chans)
    cells[1] = down(0, 0, 3) + bias
    emit(1, None)
    cells[0] = down(0, 2, 1) + bias
    arrived(8)
    emit(0, keep)
    for k in range(9):
        sent(k)


def per_device(spans, rows_n, features, lengths, order, wa, ba, wb, bb, wd, bd):
    _, frames, height, cols, chans = features.shape
    hbm = pl.BlockSpec(memory_space=pltpu.HBM)
    vmem = pl.BlockSpec(memory_space=pltpu.VMEM)
    shape = (1, frames // 2, height // 4, cols // 4, 4 * chans)
    return pl.pallas_call(
        functools.partial(kernel, spans, rows_n),
        out_shape=jax.ShapeDtypeStruct(shape, F32),
        in_specs=[hbm] * 9,
        out_specs=vmem,
        scratch_shapes=[
            pltpu.VMEM((frames + 2, 4 * GROUP + 2, cols, chans), BF16),
            pltpu.VMEM((frames + 2, 4 * GROUP, cols, chans), BF16),
            pltpu.VMEM((frames, height + 1, cols, chans), BF16),
            pltpu.VMEM((4, 3, 3, chans, 2 * chans), BF16),
            pltpu.VMEM((4, 3, 3, chans, 2 * chans), BF16),
            pltpu.VMEM((3, 3, chans, 3 * chans), BF16),
            pltpu.VMEM((chans,), F32),
            pltpu.VMEM((chans,), F32),
            pltpu.VMEM((chans,), F32),
            pltpu.SMEM(lengths.shape, jnp.int32),
            pltpu.SMEM(order.shape, jnp.int32),
            pltpu.VMEM((2, height // 2 * cols, chans), F32),
            pltpu.VMEM((height // 4 * cols, chans), F32),
            pltpu.VMEM((height // 4 * cols, chans), F32),
            pltpu.SemaphoreType.DMA((9,)),
            pltpu.SemaphoreType.DMA((9,)),
            pltpu.SemaphoreType.DMA((22,)),
        ],
        compiler_params=pltpu.CompilerParams(
            collective_id=0, has_side_effects=True, vmem_limit_bytes=64 * 1024 * 1024
        ),
    )(features, lengths, order, wa, ba, wb, bb, wd, bd).astype(BF16)


def solution(mesh):
    placed = (P("span", None, "row", None, None), P(), P(), P(), P(), P(), P(), P(), P())
    return jax.shard_map(
        functools.partial(per_device, mesh.shape["span"], mesh.shape["row"]),
        mesh=mesh,
        in_specs=placed,
        out_specs=P("span", None, "row", None, None),
        check_vma=False,
    )
```

```python
import functools

import jax
import jax.numpy as jnp
from jax import lax
from jax.experimental import pallas as pl
from jax.experimental.pallas import tpu as pltpu
from jax.sharding import PartitionSpec as P

MESH = pl.DeviceIdType.MESH
UP = 3
LOW = 2
GROUP = 3
BF16 = jnp.bfloat16
F32 = jnp.float32


def kernel(
    spans,
    rows_n,
    x_hbm,
    lengths_hbm,
    order_hbm,
    wa_hbm,
    ba_hbm,
    wb_hbm,
    bb_hbm,
    wd_hbm,
    bd_hbm,
    out,
    xs,
    hs,
    ms,
    wa,
    wb,
    wd,
    ba,
    bb,
    bd,
    lengths,
    order,
    cells,
    share,
    passed,
    send_sem,
    recv_sem,
    load_sem,
):
    s = lax.axis_index("span")
    r = lax.axis_index("row")
    height, cols, chans = x_hbm.shape[2], x_hbm.shape[3], x_hbm.shape[4]
    hid_rows = height + UP
    mix_rows = height + 1
    inner = UP + height - 2

    first_s, last_s = s == 0, s == spans - 1
    first_r, last_r = r == 0, r == rows_n - 1
    no = jnp.logical_not
    both = jnp.logical_and
    s_to, r_to, r_back = (
        jnp.minimum(s + 1, spans - 1),
        jnp.minimum(r + 1, rows_n - 1),
        jnp.maximum(r - 1, 0),
    )
    s_from = jnp.maximum(s - 1, 0)
    odd = s % 2 == 1
    even = no(odd)
    kinds = [
        ((s, r_to), no(last_r), no(first_r), (s, r_back)),
        ((s, r_back), no(first_r), no(last_r), (s, r_to)),
        ((s_to, r), no(last_s), no(first_s), (s_from, r)),
        (
            (s_to, r_to),
            both(odd, both(no(last_s), no(last_r))),
            both(even, both(no(first_s), no(first_r))),
            (s_from, r_back),
        ),
        (
            (s_to, r_back),
            both(odd, both(no(last_s), no(first_r))),
            both(even, both(no(first_s), no(last_r))),
            (s_from, r_to),
        ),
    ]

    barrier = pltpu.get_barrier_semaphore()
    for _, _, receives, sender in kinds:

        @pl.when(receives)
        def _():
            pl.semaphore_signal(barrier, inc=1, device_id=sender, device_id_type=MESH)

    used = [0]

    def load(source, target):
        copy = pltpu.make_async_copy(source, target, load_sem.at[used[0]])
        used[0] += 1
        copy.start()
        return copy

    def paired(source, target):
        return [
            load(source.at[t], target.at[t + o, :, :, :, o * chans : (o + 1) * chans])
            for t in range(3)
            for o in range(2)
        ]

    load_x = [load(x_hbm.at[0], xs.at[2:6, UP : UP + height])]
    load_a = paired(wa_hbm, wa) + [load(ba_hbm, ba)]
    load_i = [load(lengths_hbm, lengths), load(order_hbm, order)]

    def blank(target):
        zeros = jnp.zeros((3, 3, chans, chans), BF16)
        target[0, :, :, :, chans : 2 * chans] = zeros
        target[3, :, :, :, 0:chans] = zeros

    blank(wa)

    greeted = sum(sends.astype(jnp.int32) for _, sends, _, _ in kinds)
    pl.semaphore_wait(barrier, greeted)

    feats = x_hbm.at[0]
    routes = [
        (feats.at[:, height - UP : height], xs.at[2:6, 0:UP]),
        (feats.at[:, 0:LOW], xs.at[2:6, UP + height : UP + height + LOW]),
        (feats.at[2:4], xs.at[0:2, UP : UP + height]),
        (feats.at[2:4, height - UP : height], xs.at[0:2, 0:UP]),
        (feats.at[2:4, 0:LOW], xs.at[0:2, UP + height : UP + height + LOW]),
        (hs.at[4:6, UP:inner], hs.at[0:2, UP:inner]),
        (hs.at[4:6, 0:UP], hs.at[0:2, 0:UP]),
        (hs.at[4:6, inner:hid_rows], hs.at[0:2, inner:hid_rows]),
        (share, passed),
        (xs.at[4:6, 0:UP], xs.at[0:2, 0:UP]),
        (xs.at[4:6, UP + height : UP + height + LOW], xs.at[0:2, UP + height : UP + height + LOW]),
    ]
    pair = both(even, no(last_s))
    kinds = kinds + 4 * [kinds[2]]
    kinds.append(((s_to, r), both(pair, no(first_r)), both(odd, no(first_r))))
    kinds.append(((s_to, r), both(pair, no(last_r)), both(odd, no(last_r))))

    def remote(k):
        return pltpu.make_async_remote_copy(
            src_ref=routes[k][0],
            dst_ref=routes[k][1],
            send_sem=send_sem.at[k],
            recv_sem=recv_sem.at[k],
            device_id=kinds[k][0],
            device_id_type=MESH,
        )

    def send(k):
        @pl.when(kinds[k][1])
        def _():
            remote(k).start()

    def sent(k):
        @pl.when(kinds[k][1])
        def _():
            remote(k).wait_send()

    def arrived(k):
        @pl.when(kinds[k][2])
        def _():
            remote(k).wait_recv()

    for k in range(5):
        send(k)

    load_b = paired(wb_hbm, wb) + [load(bb_hbm, bb)]
    load_d = [
        load(wd_hbm.at[:, :, w], wd.at[:, :, :, w * chans : (w + 1) * chans]) for w in range(3)
    ] + [load(bd_hbm, bd)]
    blank(wb)

    @pl.when(first_s)
    def _():
        for field in (xs, hs):
            field[0:2] = jnp.zeros((2,) + field.shape[1:], BF16)
        passed[...] = jnp.zeros(passed.shape, F32)

    @pl.when(first_r)
    def _():
        xs[:, 0:UP] = jnp.zeros((6, UP, cols, chans), BF16)

    @pl.when(last_r)
    def _():
        xs[:, UP + height : UP + height + LOW] = jnp.zeros((6, LOW, cols, chans), BF16)

    spare = xs.shape[1] - (UP + height + LOW)
    xs[:, UP + height + LOW :] = jnp.zeros((6, spare, cols, chans), BF16)

    def waited(copies):
        for copy in copies:
            copy.wait()

    def shifted(y0, y1, y2):
        n, width = y1.shape
        col = lax.broadcasted_iota(jnp.int32, (n // cols, cols, width), 1).reshape(n, width)
        left = jnp.where(col == 0, 0.0, pltpu.roll(y0, 1, 0))
        right = jnp.where(col == cols - 1, 0.0, pltpu.roll(y2, n - 1, 0))
        return y1 + left + right

    def stacked(field, frame, parts):
        got = [field[frame, pl.ds(lo, n)].reshape(n * cols, chans) for lo, n in parts]
        return got[0] if len(got) == 1 else jnp.concatenate(got, axis=0)

    def conv_pair(field, base, parts, weight):
        lhs = jnp.concatenate(
            [
                stacked(field, base + f, [(lo + h, n) for lo, n in parts])
                for f in range(4)
                for h in range(3)
            ],
            axis=1,
        )
        y = [
            jnp.dot(
                lhs,
                weight[:, :, w].reshape(12 * chans, 2 * chans),
                preferred_element_type=F32,
            )
            for w in range(3)
        ]
        return shifted(*y)

    def hidden_pair(base, parts):
        y = conv_pair(xs, base, parts, wa)
        for o in range(2):
            v = y[:, o * chans : (o + 1) * chans] + ba[...].reshape(1, chans)
            v = (v / (1.0 + jnp.exp(-v))).astype(BF16)
            at = 0
            for lo, n in parts:
                hs[base + 2 + o, pl.ds(lo, n)] = v[at : at + n * cols].reshape(n, cols, chans)
                at += n * cols

    def hidden_rim(base):
        @pl.when(first_r)
        def _():
            hs[base + 2 : base + 4, 0 : UP - 1] = jnp.zeros((2, UP - 1, cols, chans), BF16)

        @pl.when(last_r)
        def _():
            hs[base + 2 : base + 4, hid_rows - 1 : hid_rows] = jnp.zeros((2, 1, cols, chans), BF16)

    def mixed_pair(base):
        y = conv_pair(hs, base, [(0, mix_rows)], wb)
        for o in range(2):
            v = y[:, o * chans : (o + 1) * chans] + bb[...].reshape(1, chans)
            x = xs[base + 2 + o, UP - 1 : UP - 1 + mix_rows].reshape(mix_rows * cols, chans)
            v = x.astype(F32) + v
            ms[base + o] = v.astype(BF16).reshape(mix_rows, cols, chans)

        @pl.when(first_r)
        def _():
            for o in range(2):
                ms[base + o, 0:1] = jnp.zeros((1, cols, chans), BF16)

    high = height // 2

    def down(base, first, count):
        lhs = jnp.concatenate(
            [
                jnp.concatenate([ms[base + t, 2 * q + h] for q in range(high)], axis=0)
                for t in range(count)
                for h in range(3)
            ],
            axis=1,
        )
        y = jnp.dot(
            lhs,
            wd[first : first + count].reshape(3 * count * chans, 3 * chans),
            preferred_element_type=F32,
        )
        return shifted(*[y[:, w * chans : (w + 1) * chans] for w in range(3)])

    def emit(j, extra):
        for i in range(high // 2):
            got = []
            for a in range(2):
                for b in range(2):
                    row = 2 * i + a
                    v = cells[j, pl.ds(row * cols + 2 * b, cols // 4, stride=4), :]
                    if extra is not None:
                        late = passed[pl.ds(row * (cols // 2) + b, cols // 4, stride=2), :]
                        v = v + late * extra
                    got.append(v)
            out[0, j, i] = jnp.concatenate(got, axis=1).astype(BF16)

    waited(load_x)
    waited(load_a)
    waited(load_i)
    start = jnp.int32(0)
    keep = jnp.int32(1)
    for i in range(lengths.shape[0]):
        keep = jnp.where(start == s, 0, keep)
        start = start + lengths[order[i]]
    keep = keep.astype(F32)

    def gate(field, lo, hi):
        block = field[0:2, lo:hi]
        field[0:2, lo:hi] = (block.astype(F32) * keep).astype(BF16)

    @pl.loop(0, 4)
    def _(i):
        @pl.when(i == 1)
        def _():
            arrived(2)
            gate(xs, UP, UP + height)

        @pl.when(i == 2)
        def _():
            for k in (0, 1):
                arrived(k)
            for k in (9, 10):
                send(k)

        @pl.when(i == 3)
        def _():
            for k in (3, 4, 9, 10):
                arrived(k)
            gate(xs, 0, UP)
            gate(xs, UP + height, UP + height + LOW)

        outer = i // 2
        low = UP - GROUP * outer
        up = UP + GROUP + GROUP * outer
        hidden_pair(2 - 2 * (i % 2), [(low, GROUP), (up, GROUP)])

        @pl.when(i == 0)
        def _():
            send(5)

        @pl.when(i == 2)
        def _():
            hidden_rim(2)
            send(6)
            send(7)

        @pl.when(i == 3)
        def _():
            hidden_rim(0)

    waited(load_b)

    @pl.loop(0, 2)
    def _(i):
        @pl.when(i == 1)
        def _():
            for k in (5, 6, 7):
                arrived(k)
            gate(hs, 0, hid_rows)

        mixed_pair(2 - 2 * i)

        @pl.when(i == 0)
        def _():
            waited(load_d)
            cells[0] = down(2, 0, 2)
            share[...] = cells[0, pl.ds(0, high * cols // 2, stride=2), :]
            send(8)

    bias = bd[...].reshape(1, chans)
    cells[1] = down(0, 0, 3) + bias
    emit(1, None)
    cells[0] = down(0, 2, 1) + bias
    arrived(8)
    emit(0, keep)
    for k in range(11):
        sent(k)


def per_device(spans, rows_n, features, lengths, order, wa, ba, wb, bb, wd, bd):
    _, frames, height, cols, chans = features.shape
    hbm = pl.BlockSpec(memory_space=pltpu.HBM)
    vmem = pl.BlockSpec(memory_space=pltpu.VMEM)
    shape = (1, frames // 2, height // 4, cols // 4, 4 * chans)
    return pl.pallas_call(
        functools.partial(kernel, spans, rows_n),
        out_shape=jax.ShapeDtypeStruct(shape, BF16),
        in_specs=[hbm] * 9,
        out_specs=vmem,
        scratch_shapes=[
            pltpu.VMEM((frames + 2, 4 * GROUP + 2, cols, chans), BF16),
            pltpu.VMEM((frames + 2, 4 * GROUP, cols, chans), BF16),
            pltpu.VMEM((frames, height + 1, cols, chans), BF16),
            pltpu.VMEM((4, 3, 3, chans, 2 * chans), BF16),
            pltpu.VMEM((4, 3, 3, chans, 2 * chans), BF16),
            pltpu.VMEM((3, 3, chans, 3 * chans), BF16),
            pltpu.VMEM((chans,), F32),
            pltpu.VMEM((chans,), F32),
            pltpu.VMEM((chans,), F32),
            pltpu.SMEM(lengths.shape, jnp.int32),
            pltpu.SMEM(order.shape, jnp.int32),
            pltpu.VMEM((2, height // 2 * cols, chans), F32),
            pltpu.VMEM((height // 4 * cols, chans), F32),
            pltpu.VMEM((height // 4 * cols, chans), F32),
            pltpu.SemaphoreType.DMA((11,)),
            pltpu.SemaphoreType.DMA((11,)),
            pltpu.SemaphoreType.DMA((22,)),
        ],
        compiler_params=pltpu.CompilerParams(
            collective_id=0, has_side_effects=True, vmem_limit_bytes=64 * 1024 * 1024
        ),
    )(features, lengths, order, wa, ba, wb, bb, wd, bd)


def solution(mesh):
    placed = (P("span", None, "row", None, None), P(), P(), P(), P(), P(), P(), P(), P())
    return jax.shard_map(
        functools.partial(per_device, mesh.shape["span"], mesh.shape["row"]),
        mesh=mesh,
        in_specs=placed,
        out_specs=P("span", None, "row", None, None),
        check_vma=False,
    )
```

```python
import functools

import jax
import jax.numpy as jnp
from jax import lax
from jax.experimental import pallas as pl
from jax.experimental.pallas import tpu as pltpu
from jax.sharding import PartitionSpec as P

MESH = pl.DeviceIdType.MESH
UP = 3
LOW = 2
GROUP = 3
BF16 = jnp.bfloat16
F32 = jnp.float32


def kernel(
    spans,
    rows_n,
    x_hbm,
    lengths_hbm,
    order_hbm,
    wa_hbm,
    ba_hbm,
    wb_hbm,
    bb_hbm,
    wd_hbm,
    bd_hbm,
    out,
    xs,
    hs,
    ms,
    wa,
    wb,
    wd,
    ba,
    bb,
    bd,
    lengths,
    order,
    cells,
    share,
    passed,
    send_sem,
    recv_sem,
    load_sem,
):
    s = lax.axis_index("span")
    r = lax.axis_index("row")
    height, cols, chans = x_hbm.shape[2], x_hbm.shape[3], x_hbm.shape[4]
    hid_rows = height + UP
    mix_rows = height + 1
    inner = UP + height - 2

    first_s, last_s = s == 0, s == spans - 1
    first_r, last_r = r == 0, r == rows_n - 1
    no = jnp.logical_not
    both = jnp.logical_and
    s_to, r_to, r_back = (
        jnp.minimum(s + 1, spans - 1),
        jnp.minimum(r + 1, rows_n - 1),
        jnp.maximum(r - 1, 0),
    )
    s_from = jnp.maximum(s - 1, 0)
    odd = s % 2 == 1
    even = no(odd)
    kinds = [
        ((s, r_to), no(last_r), no(first_r), (s, r_back)),
        ((s, r_back), no(first_r), no(last_r), (s, r_to)),
        ((s_to, r), no(last_s), no(first_s), (s_from, r)),
        (
            (s_to, r_to),
            both(odd, both(no(last_s), no(last_r))),
            both(even, both(no(first_s), no(first_r))),
            (s_from, r_back),
        ),
        (
            (s_to, r_back),
            both(odd, both(no(last_s), no(first_r))),
            both(even, both(no(first_s), no(last_r))),
            (s_from, r_to),
        ),
    ]

    barrier = pltpu.get_barrier_semaphore()
    for _, _, receives, sender in kinds:

        @pl.when(receives)
        def _():
            pl.semaphore_signal(barrier, inc=1, device_id=sender, device_id_type=MESH)

    used = [0]

    def load(source, target):
        copy = pltpu.make_async_copy(source, target, load_sem.at[used[0]])
        used[0] += 1
        copy.start()
        return copy

    def paired(source, target):
        return [
            load(source.at[t], target.at[t + o, :, :, :, o * chans : (o + 1) * chans])
            for t in range(3)
            for o in range(2)
        ]

    load_x = [load(x_hbm.at[0], xs.at[2:6, UP : UP + height])]
    load_a = paired(wa_hbm, wa) + [load(ba_hbm, ba)]
    load_i = [load(lengths_hbm, lengths), load(order_hbm, order)]

    def blank(target):
        zeros = jnp.zeros((3, 3, chans, chans), BF16)
        target[0, :, :, :, chans : 2 * chans] = zeros
        target[3, :, :, :, 0:chans] = zeros

    blank(wa)

    greeted = sum(sends.astype(jnp.int32) for _, sends, _, _ in kinds)
    pl.semaphore_wait(barrier, greeted)

    feats = x_hbm.at[0]
    routes = [
        (feats.at[:, height - UP : height], xs.at[2:6, 0:UP]),
        (feats.at[:, 0:LOW], xs.at[2:6, UP + height : UP + height + LOW]),
        (feats.at[2:4], xs.at[0:2, UP : UP + height]),
        (feats.at[2:4, height - UP : height], xs.at[0:2, 0:UP]),
        (feats.at[2:4, 0:LOW], xs.at[0:2, UP + height : UP + height + LOW]),
        (hs.at[4:6, UP:inner], hs.at[0:2, UP:inner]),
        (hs.at[4:6, 0:UP], hs.at[0:2, 0:UP]),
        (hs.at[4:6, inner:hid_rows], hs.at[0:2, inner:hid_rows]),
        (share, passed),
        (xs.at[4:6, 0:UP], xs.at[0:2, 0:UP]),
        (xs.at[4:6, UP + height : UP + height + LOW], xs.at[0:2, UP + height : UP + height + LOW]),
    ]
    pair = both(even, no(last_s))
    kinds = kinds + 4 * [kinds[2]]
    kinds.append(((s_to, r), both(pair, no(first_r)), both(odd, no(first_r))))
    kinds.append(((s_to, r), both(pair, no(last_r)), both(odd, no(last_r))))

    def remote(k):
        return pltpu.make_async_remote_copy(
            src_ref=routes[k][0],
            dst_ref=routes[k][1],
            send_sem=send_sem.at[k],
            recv_sem=recv_sem.at[k],
            device_id=kinds[k][0],
            device_id_type=MESH,
        )

    def send(k):
        @pl.when(kinds[k][1])
        def _():
            remote(k).start()

    def sent(k):
        @pl.when(kinds[k][1])
        def _():
            remote(k).wait_send()

    def arrived(k):
        @pl.when(kinds[k][2])
        def _():
            remote(k).wait_recv()

    for k in (2, 0, 1, 3, 4):
        send(k)

    load_b = paired(wb_hbm, wb) + [load(bb_hbm, bb)]
    load_d = [
        load(wd_hbm.at[:, :, w], wd.at[:, :, :, w * chans : (w + 1) * chans]) for w in range(3)
    ] + [load(bd_hbm, bd)]
    blank(wb)

    @pl.when(first_s)
    def _():
        for field in (xs, hs):
            field[0:2] = jnp.zeros((2,) + field.shape[1:], BF16)
        passed[...] = jnp.zeros(passed.shape, F32)

    @pl.when(first_r)
    def _():
        xs[:, 0:UP] = jnp.zeros((6, UP, cols, chans), BF16)

    @pl.when(last_r)
    def _():
        xs[:, UP + height : UP + height + LOW] = jnp.zeros((6, LOW, cols, chans), BF16)

    spare = xs.shape[1] - (UP + height + LOW)
    xs[:, UP + height + LOW :] = jnp.zeros((6, spare, cols, chans), BF16)

    def waited(copies):
        for copy in copies:
            copy.wait()

    def shifted(y0, y1, y2):
        n, width = y1.shape
        col = lax.broadcasted_iota(jnp.int32, (n // cols, cols, width), 1).reshape(n, width)
        left = jnp.where(col == 0, 0.0, pltpu.roll(y0, 1, 0))
        right = jnp.where(col == cols - 1, 0.0, pltpu.roll(y2, n - 1, 0))
        return y1 + left + right

    def stacked(field, frame, parts):
        got = [field[frame, pl.ds(lo, n)].reshape(n * cols, chans) for lo, n in parts]
        return got[0] if len(got) == 1 else jnp.concatenate(got, axis=0)

    def conv_pair(field, base, parts, weight):
        lhs = jnp.concatenate(
            [
                stacked(field, base + f, [(lo + h, n) for lo, n in parts])
                for f in range(4)
                for h in range(3)
            ],
            axis=1,
        )
        y = [
            jnp.dot(
                lhs,
                weight[:, :, w].reshape(12 * chans, 2 * chans),
                preferred_element_type=F32,
            )
            for w in range(3)
        ]
        return shifted(*y)

    def hidden_pair(base, parts):
        y = conv_pair(xs, base, parts, wa)
        for o in range(2):
            v = y[:, o * chans : (o + 1) * chans] + ba[...].reshape(1, chans)
            v = (v / (1.0 + jnp.exp(-v))).astype(BF16)
            at = 0
            for lo, n in parts:
                hs[base + 2 + o, pl.ds(lo, n)] = v[at : at + n * cols].reshape(n, cols, chans)
                at += n * cols

    def hidden_rim(base):
        @pl.when(first_r)
        def _():
            hs[base + 2 : base + 4, 0 : UP - 1] = jnp.zeros((2, UP - 1, cols, chans), BF16)

        @pl.when(last_r)
        def _():
            hs[base + 2 : base + 4, hid_rows - 1 : hid_rows] = jnp.zeros((2, 1, cols, chans), BF16)

    def mixed_pair(base):
        y = conv_pair(hs, base, [(0, mix_rows)], wb)
        for o in range(2):
            v = y[:, o * chans : (o + 1) * chans] + bb[...].reshape(1, chans)
            x = xs[base + 2 + o, UP - 1 : UP - 1 + mix_rows].reshape(mix_rows * cols, chans)
            v = x.astype(F32) + v
            ms[base + o] = v.astype(BF16).reshape(mix_rows, cols, chans)

        @pl.when(first_r)
        def _():
            for o in range(2):
                ms[base + o, 0:1] = jnp.zeros((1, cols, chans), BF16)

    high = height // 2

    def down(base, first, count):
        lhs = jnp.concatenate(
            [
                jnp.concatenate([ms[base + t, 2 * q + h] for q in range(high)], axis=0)
                for t in range(count)
                for h in range(3)
            ],
            axis=1,
        )
        y = jnp.dot(
            lhs,
            wd[first : first + count].reshape(3 * count * chans, 3 * chans),
            preferred_element_type=F32,
        )
        return shifted(*[y[:, w * chans : (w + 1) * chans] for w in range(3)])

    def emit(j, extra):
        for i in range(high // 2):
            got = []
            for a in range(2):
                for b in range(2):
                    row = 2 * i + a
                    v = cells[j, pl.ds(row * cols + 2 * b, cols // 4, stride=4), :]
                    if extra is not None:
                        late = passed[pl.ds(row * (cols // 2) + b, cols // 4, stride=2), :]
                        v = v + late * extra
                    got.append(v)
            out[0, j, i] = jnp.concatenate(got, axis=1).astype(BF16)

    waited(load_x)
    waited(load_a)
    waited(load_i)
    start = jnp.int32(0)
    keep = jnp.int32(1)
    for i in range(lengths.shape[0]):
        keep = jnp.where(start == s, 0, keep)
        start = start + lengths[order[i]]
    keep = keep.astype(F32)

    def gate(field, lo, hi):
        block = field[0:2, lo:hi]
        field[0:2, lo:hi] = (block.astype(F32) * keep).astype(BF16)

    @pl.loop(0, 4)
    def _(i):
        @pl.when(i == 1)
        def _():
            arrived(2)
            gate(xs, UP, UP + height)

        @pl.when(i == 2)
        def _():
            for k in (0, 1):
                arrived(k)
            for k in (9, 10):
                send(k)

        @pl.when(i == 3)
        def _():
            for k in (3, 4, 9, 10):
                arrived(k)
            gate(xs, 0, UP)
            gate(xs, UP + height, UP + height + LOW)

        outer = i // 2
        low = UP - GROUP * outer
        up = UP + GROUP + GROUP * outer
        hidden_pair(2 - 2 * (i % 2), [(low, GROUP), (up, GROUP)])

        @pl.when(i == 0)
        def _():
            send(5)

        @pl.when(i == 2)
        def _():
            hidden_rim(2)
            send(6)
            send(7)

        @pl.when(i == 3)
        def _():
            hidden_rim(0)

    waited(load_b)

    @pl.loop(0, 2)
    def _(i):
        @pl.when(i == 1)
        def _():
            for k in (5, 6, 7):
                arrived(k)
            gate(hs, 0, hid_rows)

        mixed_pair(2 - 2 * i)

        @pl.when(i == 0)
        def _():
            waited(load_d)
            cells[0] = down(2, 0, 2)
            share[...] = cells[0, pl.ds(0, high * cols // 2, stride=2), :]
            send(8)

    bias = bd[...].reshape(1, chans)
    cells[1] = down(0, 0, 3) + bias
    emit(1, None)
    cells[0] = down(0, 2, 1) + bias
    arrived(8)
    emit(0, keep)
    for k in range(11):
        sent(k)


def per_device(spans, rows_n, features, lengths, order, wa, ba, wb, bb, wd, bd):
    _, frames, height, cols, chans = features.shape
    hbm = pl.BlockSpec(memory_space=pltpu.HBM)
    vmem = pl.BlockSpec(memory_space=pltpu.VMEM)
    shape = (1, frames // 2, height // 4, cols // 4, 4 * chans)
    return pl.pallas_call(
        functools.partial(kernel, spans, rows_n),
        out_shape=jax.ShapeDtypeStruct(shape, BF16),
        in_specs=[hbm] * 9,
        out_specs=vmem,
        scratch_shapes=[
            pltpu.VMEM((frames + 2, 4 * GROUP + 2, cols, chans), BF16),
            pltpu.VMEM((frames + 2, 4 * GROUP, cols, chans), BF16),
            pltpu.VMEM((frames, height + 1, cols, chans), BF16),
            pltpu.VMEM((4, 3, 3, chans, 2 * chans), BF16),
            pltpu.VMEM((4, 3, 3, chans, 2 * chans), BF16),
            pltpu.VMEM((3, 3, chans, 3 * chans), BF16),
            pltpu.VMEM((chans,), F32),
            pltpu.VMEM((chans,), F32),
            pltpu.VMEM((chans,), F32),
            pltpu.SMEM(lengths.shape, jnp.int32),
            pltpu.SMEM(order.shape, jnp.int32),
            pltpu.VMEM((2, height // 2 * cols, chans), F32),
            pltpu.VMEM((height // 4 * cols, chans), F32),
            pltpu.VMEM((height // 4 * cols, chans), F32),
            pltpu.SemaphoreType.DMA((11,)),
            pltpu.SemaphoreType.DMA((11,)),
            pltpu.SemaphoreType.DMA((22,)),
        ],
        compiler_params=pltpu.CompilerParams(
            collective_id=0, has_side_effects=True, vmem_limit_bytes=64 * 1024 * 1024
        ),
    )(features, lengths, order, wa, ba, wb, bb, wd, bd)


def solution(mesh):
    placed = (P("span", None, "row", None, None), P(), P(), P(), P(), P(), P(), P(), P())
    return jax.shard_map(
        functools.partial(per_device, mesh.shape["span"], mesh.shape["row"]),
        mesh=mesh,
        in_specs=placed,
        out_specs=P("span", None, "row", None, None),
        check_vma=False,
    )
```
